256 devices in a mesh: pool: 2 (over y_hi), fsdp: 64 (over z, y_lo, x), rep: 2 (over core).
Axes of the slice: x: 4, y: 4 (y_hi: 2, y_lo: 2; y = y_hi * 2 + y_lo), z: 8, core: 2. Of those that a mesh axis runs over, the one named last changes fastest.
Arguments:
- master: float32 [6144, 16384], P(('pool', 'fsdp', 'rep')), may hold values from -6 to 6
- grad: bfloat16 [6144, 16384], P(('pool', 'fsdp', 'rep')), may hold values from -6 to 6
- first_moment: float32 [6144, 16384], P(('pool', 'fsdp', 'rep')), may hold values from -6 to 6
- second_moment: float32 [6144, 16384], P(('pool', 'fsdp', 'rep')), may hold values from 0.05 to 2
- matching: int32 [64], replicated, may hold values from 0 to 63, each once
Outputs:
- new_master: float32 [6144, 16384], P(('pool', 'fsdp', 'rep'))
- new_first: float32 [6144, 16384], P(('pool', 'fsdp', 'rep'))
- new_second: float32 [6144, 16384], P(('pool', 'fsdp', 'rep'))
- rollout_weight: bfloat16 [64, 6144, 256], P('fsdp')
The draws below stay inside these ranges and needn't reach their ends.
Inputs may be any that keep to these rules, and one draw needn't show every extreme that they name: matching is a permutation: rollout rank r is hosted at fsdp index matching[r].
All inputs are finite; a program needn't handle non-finite values.
Results may differ from the reference program's by a relative error of at most 0.001.
Values may be sent and summed in bfloat16 or wider, within the bound.
A program may use at most 64 MiB of HBM per device.

```python
import math
import jax
import jax.numpy as jnp
from jax import lax

D = 6144
FF = 16384
N_FSDP = 64


def block_scale(key, extent, shards, low, largest):
    gain = 1.0
    for dim, parts in shards:
        draws = jax.random.uniform(jax.random.fold_in(jax.random.fold_in(key, 6), dim), (parts,), jnp.float32, low / len(shards), largest / len(shards))
        gain = gain * jnp.repeat(jnp.exp(draws), extent[dim] // parts).reshape((-1,) + (1,) * (len(extent) - 1 - dim))
    return gain


def bell_draw(key, extent, scale, bound, cuts=(), held_as=jnp.bfloat16):
    values = scale * jax.random.normal(key, extent, jnp.float32)
    if cuts:
        values = values * block_scale(key, extent, cuts, -0.22, 0.18)
    return jnp.clip(values, -bound, bound).astype(held_as)


def setup_inputs(seed: int = 0) -> dict:
    streams_of = jax.random.split(jax.random.key(seed), 6)
    return {
        "master": bell_draw(streams_of[0], (D, FF), 1.0, 6.0, ((0, 256),), jnp.float32),
        "grad": bell_draw(streams_of[1], (D, FF), 1.0, 6.0, ((0, 256),)),
        "first_moment": bell_draw(streams_of[2], (D, FF), 0.5, 6.0, ((0, 256),), jnp.float32),
        "second_moment": jnp.clip(jnp.exp(math.log(2.0) - 3.6888794 * jax.random.uniform(streams_of[3], (D, FF), jnp.float32) ** block_scale(streams_of[3], (D, FF), ((0, 256),), -0.2, 0.2)), 0.05, 2.0),
        "matching": jax.random.permutation(streams_of[4], N_FSDP).astype(jnp.int32),
    }


beta_one = 0.9
beta_two = 0.95
learn_rate = 0.05
decay_rate = 0.1
epsilon = 1e-08
bias_one = 1.0 - 0.9 ** 10
bias_two = 1.0 - 0.95 ** 10

def adamw_step(master, grad, first_moment, second_moment):
    gradient = grad.astype(jnp.float32)
    new_first = beta_one * first_moment + (1.0 - beta_one) * gradient
    new_second = beta_two * second_moment + (1.0 - beta_two) * gradient * gradient
    update = new_first / bias_one / (jnp.sqrt(new_second / bias_two) + epsilon)
    new_master = master * (1.0 - learn_rate * decay_rate) - learn_rate * update
    return (new_master, new_first, new_second)

def reference(master, grad, first_moment, second_moment, matching):
    new_master, new_first, new_second = adamw_step(master, grad, first_moment, second_moment)
    weights = new_master.astype(jnp.bfloat16)
    count = matching.shape[0]
    inverse = jnp.zeros((count,), jnp.int32).at[matching.astype(jnp.int32)].set(lax.iota(jnp.int32, count))
    blocks = weights.reshape(D, count, FF // count).transpose(1, 0, 2)
    rollout_weight = jnp.take(blocks, inverse, axis=0)
    return (new_master, new_first, new_second, rollout_weight)
```

```python
import functools

import jax
import jax.numpy as jnp
from jax import lax
from jax.experimental import pallas as pl
from jax.experimental.pallas import tpu as pltpu
from jax.sharding import PartitionSpec as P

MESH = pl.DeviceIdType.MESH
beta_one = 0.9
beta_two = 0.95
learn_rate = 0.05
decay_rate = 0.1
epsilon = 1e-08
bias_one = 1.0 - 0.9**10
bias_two = 1.0 - 0.95**10

NX, NY, NZ = 4, 4, 8
STEPS = NX * NZ
GROUP = NX
GROUPS = STEPS // GROUP
CHUNKS = 8
LAG = 3


def place():
    pool, fsdp, core = lax.axis_index("pool"), lax.axis_index("fsdp"), lax.axis_index("rep")
    return fsdp % NX, pool * 2 + (fsdp // NX) % 2, fsdp // (2 * NX), core


def device(x, y, z, core):
    x, y, z, core = (x + NX) % NX, (y + NY) % NY, (z + NZ) % NZ, core % 2
    return (y // 2, z * (2 * NX) + (y % 2) * NX + x, core)


def offset(k):
    j = k // NX
    return k % NX, ((j + 1) // 2) * (2 * (j % 2) - 1)


def adamw(master, grad, first, second):
    gradient = grad.astype(jnp.float32)
    new_first = beta_one * first + (1.0 - beta_one) * gradient
    new_second = beta_two * second + (1.0 - beta_two) * gradient * gradient
    step = new_first * (learn_rate / bias_one)
    new_master = master * (1.0 - learn_rate * decay_rate) - step / (jnp.sqrt(new_second * (1.0 / bias_two)) + epsilon)
    return new_master, new_first, new_second


def kernel(
    master_hbm, grad_hbm, first_hbm, second_hbm, matching_ref,
    new_master, new_first, new_second, rollout,
    master, grad, first, second, weights, row, ranks, packed, held,
    in_sem, rank_sem, plane_send, plane_recv, y_send, y_recv, core_send, core_recv,
):
    rows, width = master.shape
    count = matching_ref.shape[1]
    cols = width // count
    half = cols // 2
    x, y, z, core = place()
    other = device(x, y, z, core + 1)

    grad_load = pltpu.make_async_copy(grad_hbm, grad, in_sem.at[0, 0])
    grad_load.start()

    def load(t, i):
        where = pl.ds(t * (width // CHUNKS), width // CHUNKS)
        src, dst = ((master_hbm, master), (first_hbm, first), (second_hbm, second))[i]
        return pltpu.make_async_copy(src.at[:, where], dst.at[:, where], in_sem.at[1 + i, t])

    for t in range(CHUNKS):
        for i in range(3):
            load(t, i).start()

    barrier = pltpu.get_barrier_semaphore()

    def greet(k, carry):
        dx, dz = offset(k)
        pl.semaphore_signal(barrier, inc=1, device_id=device(x + dx, y, z + dz, core), device_id_type=MESH)
        return carry

    lax.fori_loop(1, STEPS, greet, 0)
    for dy in (1, 2, 3):
        pl.semaphore_signal(barrier, inc=1, device_id=device(x, y + dy, z, core), device_id_type=MESH)
    pl.semaphore_signal(barrier, inc=1, device_id=other, device_id_type=MESH)

    lane = lax.broadcasted_iota(jnp.int32, (count, count), 1)
    sub = lax.broadcasted_iota(jnp.int32, (count, count), 0)
    hit = jnp.where(matching_ref[...] == sub, lane, 0)
    column = jnp.max(hit, axis=1, keepdims=True)
    row[...] = jnp.sum(jnp.where(lane == sub, column, 0), axis=0, keepdims=True)
    to_scalar = pltpu.make_async_copy(row, ranks, rank_sem)
    to_scalar.start()
    to_scalar.wait()
    grad_load.wait()
    for t in range(CHUNKS):
        for i in range(3):
            load(t, i).wait()

        def block(n, carry):
            where = pl.ds(pl.multiple_of(n * cols, cols), cols)
            value, new_first[:, where], new_second[:, where] = adamw(
                master[:, where], grad[:, where], first[:, where], second[:, where]
            )
            new_master[:, where] = value
            weights[n] = jnp.concatenate([value[:, :half], value[:, half:]], axis=0).astype(jnp.bfloat16)
            return carry

        lax.fori_loop(t * (count // CHUNKS), (t + 1) * (count // CHUNKS), block, 0)

    def piece(dx, dz, parity):
        host = ((z + NZ + dz) % NZ) * (2 * NX) + ((y + parity) % 2) * NX + (x + dx) % NX
        return weights[ranks[0, host]]

    held[core, 0, 0] = piece(0, 0, 1)
    held[core, 1, 0] = piece(0, 0, 0)
    pl.semaphore_wait(barrier, STEPS - 1 + 3 + 1)

    def send(k, carry):
        dx, dz = offset(k)
        packed[k, 0] = piece(dx, dz, 1)
        packed[k, 1] = piece(dx, dz, 0)
        pltpu.make_async_remote_copy(
            src_ref=packed.at[k],
            dst_ref=held.at[core, pl.ds(0, 2), k],
            send_sem=plane_send,
            recv_sem=plane_recv.at[k // GROUP],
            device_id=device(x + dx, y, z + dz, core),
            device_id_type=MESH,
        ).start()
        return carry

    lax.fori_loop(1, STEPS, send, 0)

    def arrived(g):
        low = max(g * GROUP, 1)
        where = held.at[core, pl.ds(0, 2), pl.ds(low, (g + 1) * GROUP - low)]
        return pltpu.make_async_remote_copy(
            src_ref=where, dst_ref=where, send_sem=plane_send, recv_sem=plane_recv.at[g], device_id=other, device_id_type=MESH
        )

    def over_y(g, dy):
        here = pl.ds(g * GROUP, GROUP)
        return pltpu.make_async_remote_copy(
            src_ref=held.at[core, 1 if dy == 2 else 0, here],
            dst_ref=held.at[core, 1 + dy, here],
            send_sem=y_send.at[dy - 1],
            recv_sem=y_recv.at[dy - 1, g],
            device_id=device(x, y + dy, z, core),
            device_id_type=MESH,
        )

    def over_chip(g):
        where = held.at[core, pl.ds(1, 4), pl.ds(g * GROUP, GROUP)]
        return pltpu.make_async_remote_copy(
            src_ref=where, dst_ref=where, send_sem=core_send, recv_sem=core_recv.at[g], device_id=other, device_id_type=MESH
        )

    def assemble(g):
        def block(n, carry):
            i, k = n // GROUP, g * GROUP + n % GROUP
            dx, dz = offset(k)
            pool, fsdp, _ = device(x + NX - dx, y + NY - i, z + NZ - dz, 0)
            start = pl.multiple_of((pool * count + fsdp) * (2 * rows), 2 * rows)
            parts = []
            for c in (0, 1):
                value = held[c, 1 + i, k].astype(jnp.float32)
                parts.append(jnp.concatenate([value[:rows], value[rows:]], axis=1))
            rollout[pl.ds(start, 2 * rows), :] = jnp.concatenate(parts, axis=0).astype(jnp.bfloat16)
            return carry

        lax.fori_loop(0, 4 * GROUP, block, 0)

    for t in range(GROUPS + LAG + 1):
        if t < GROUPS:
            arrived(t).wait_recv()
            for dy in (1, 2, 3):
                over_y(t, dy).start()
        if 0 <= t - LAG < GROUPS:
            for dy in (1, 2, 3):
                over_y(t - LAG, dy).wait_recv()
            over_chip(t - LAG).start()
        if 0 <= t - LAG - 1 < GROUPS:
            over_chip(t - LAG - 1).wait_recv()
            assemble(t - LAG - 1)

    def drain(ref, sem):
        pltpu.make_async_remote_copy(
            src_ref=ref, dst_ref=ref, send_sem=sem, recv_sem=plane_recv.at[0], device_id=other, device_id_type=MESH
        ).wait_send()

    drain(packed.at[pl.ds(1, STEPS - 1)], plane_send)
    for dy in (1, 2, 3):
        drain(held.at[core, 1 if dy == 2 else 0], y_send.at[dy - 1])
    drain(held.at[core, pl.ds(1, 4)], core_send)


def per_device(master, grad, first_moment, second_moment, matching):
    rows, width = master.shape
    count = matching.shape[0]
    cols = width // count
    total = 2 * count * 2 * rows
    hbm = pl.BlockSpec(memory_space=pltpu.HBM)
    vmem = pl.BlockSpec(memory_space=pltpu.VMEM)
    dma = pltpu.SemaphoreType.DMA
    new_master, new_first, new_second, rollout = pl.pallas_call(
        kernel,
        out_shape=[pltpu.VMEM((rows, width), jnp.float32)] * 3 + [pltpu.VMEM((total, cols), jnp.bfloat16)],
        in_specs=[hbm] * 4 + [vmem],
        out_specs=[vmem] * 4,
        scratch_shapes=[
            pltpu.VMEM((rows, width), jnp.float32),
            pltpu.VMEM((rows, width), jnp.bfloat16),
            pltpu.VMEM((rows, width), jnp.float32),
            pltpu.VMEM((rows, width), jnp.float32),
            pltpu.VMEM((count, 2 * rows, cols // 2), jnp.bfloat16),
            pltpu.VMEM((1, count), jnp.int32),
            pltpu.SMEM((1, count), jnp.int32),
            pltpu.VMEM((STEPS, 2, 2 * rows, cols // 2), jnp.bfloat16),
            pltpu.VMEM((2, 5, STEPS, 2 * rows, cols // 2), jnp.bfloat16),
            dma((4, CHUNKS)),
            dma,
            dma,
            dma((GROUPS,)),
            dma((3,)),
            dma((3, GROUPS)),
            dma,
            dma((GROUPS,)),
        ],
        compiler_params=pltpu.CompilerParams(collective_id=0, has_side_effects=True, vmem_limit_bytes=30 << 20),
    )(master, grad, first_moment, second_moment, matching.reshape(1, count))
    return new_master, new_first, new_second, rollout.reshape(1, total, cols)


def solution(mesh):
    rows = P(("pool", "fsdp", "rep"), None)
    return jax.shard_map(
        per_device,
        mesh=mesh,
        in_specs=(rows, rows, rows, rows, P()),
        out_specs=(rows, rows, rows, P("fsdp", None, None)),
        check_vma=False,
    )
```

```python
import functools

import jax
import jax.numpy as jnp
from jax import lax
from jax.experimental import pallas as pl
from jax.experimental.pallas import tpu as pltpu
from jax.sharding import PartitionSpec as P

MESH = pl.DeviceIdType.MESH
beta_one = 0.9
beta_two = 0.95
learn_rate = 0.05
decay_rate = 0.1
epsilon = 1e-08
bias_one = 1.0 - 0.9**10
bias_two = 1.0 - 0.95**10

NX, NY, NZ = 4, 4, 8
STEPS = NX * NZ
GROUPS = (
    (0, 4, 3.0), (4, 4, 6.0), (8, 4, 6.2), (12, 4, 10.0), (16, 4, 10.2),
    (20, 2, 12.5), (24, 2, 12.7), (22, 2, 15.0), (26, 2, 15.2),
    (28, 1, 15.6), (29, 1, 17.0), (30, 1, 18.5), (31, 1, 19.5),
)
Y_TIME, CHIP_TIME = 3.5, 1.5
CHUNKS = 8


def place():
    pool, fsdp, core = lax.axis_index("pool"), lax.axis_index("fsdp"), lax.axis_index("rep")
    return fsdp % NX, pool * 2 + (fsdp // NX) % 2, fsdp // (2 * NX), core


def device(x, y, z, core):
    x, y, z, core = (x + NX) % NX, (y + NY) % NY, (z + NZ) % NZ, core % 2
    return (y // 2, z * (2 * NX) + (y % 2) * NX + x, core)


def offset(k):
    j = k // NX
    return k % NX, ((j + 1) // 2) * (2 * (j % 2) - 1)


def adamw(master, grad, first, second):
    gradient = grad.astype(jnp.float32)
    new_first = beta_one * first + (1.0 - beta_one) * gradient
    new_second = beta_two * second + (1.0 - beta_two) * gradient * gradient
    step = new_first * (learn_rate / bias_one)
    new_master = master * (1.0 - learn_rate * decay_rate) - step / (jnp.sqrt(new_second * (1.0 / bias_two)) + epsilon)
    return new_master, new_first, new_second


def kernel(
    master_hbm, grad_hbm, first_hbm, second_hbm, matching_hbm,
    new_master, new_first, new_second, rollout,
    master, grad, first, second, weights, matching, row, ranks, packed, held,
    in_sem, rank_sem, plane_send, plane_recv, y_send, y_recv, core_send, core_recv,
):
    rows, width = master.shape
    count = matching_hbm.shape[1]
    cols = width // count
    half = cols // 2
    x, y, z, core = place()
    other = device(x, y, z, core + 1)

    matching_load = pltpu.make_async_copy(matching_hbm, matching, rank_sem)
    matching_load.start()
    grad_load = pltpu.make_async_copy(grad_hbm, grad, in_sem.at[0, 0])
    grad_load.start()

    def load(t, i):
        where = pl.ds(t * (width // CHUNKS), width // CHUNKS)
        src, dst = ((master_hbm, master), (first_hbm, first), (second_hbm, second))[i]
        return pltpu.make_async_copy(src.at[:, where], dst.at[:, where], in_sem.at[1 + i, t])

    for t in range(CHUNKS):
        for i in range(3):
            load(t, i).start()

    barrier = pltpu.get_barrier_semaphore()

    def greet(k, carry):
        dx, dz = offset(k)
        pl.semaphore_signal(barrier, inc=1, device_id=device(x + dx, y, z + dz, core), device_id_type=MESH)
        return carry

    lax.fori_loop(1, STEPS, greet, 0)
    for dy in (1, 2, 3):
        pl.semaphore_signal(barrier, inc=1, device_id=device(x, y + dy, z, core), device_id_type=MESH)
    pl.semaphore_signal(barrier, inc=1, device_id=other, device_id_type=MESH)

    matching_load.wait()
    lane = lax.broadcasted_iota(jnp.int32, (count, count), 1)
    sub = lax.broadcasted_iota(jnp.int32, (count, count), 0)
    hit = jnp.where(matching[...] == sub, lane, 0)
    column = jnp.max(hit, axis=1, keepdims=True)
    row[...] = jnp.sum(jnp.where(lane == sub, column, 0), axis=0, keepdims=True)
    to_scalar = pltpu.make_async_copy(row, ranks, rank_sem)
    to_scalar.start()
    to_scalar.wait()
    grad_load.wait()
    for t in range(CHUNKS):
        for i in range(3):
            load(t, i).wait()

        def block(n, carry):
            where = pl.ds(pl.multiple_of(n * cols, cols), cols)
            value, new_first[:, where], new_second[:, where] = adamw(
                master[:, where], grad[:, where], first[:, where], second[:, where]
            )
            new_master[:, where] = value
            weights[n] = jnp.concatenate([value[:, :half], value[:, half:]], axis=0).astype(jnp.bfloat16)
            return carry

        lax.fori_loop(t * (count // CHUNKS), (t + 1) * (count // CHUNKS), block, 0)

    def piece(dx, dz, parity):
        host = ((z + NZ + dz) % NZ) * (2 * NX) + ((y + parity) % 2) * NX + (x + dx) % NX
        return weights[ranks[0, host]]

    held[core, 0, 0] = piece(0, 0, 1)
    held[core, 1, 0] = piece(0, 0, 0)
    pl.semaphore_wait(barrier, STEPS - 1 + 3 + 1)

    def sender(g):
        def send(k, carry):
            dx, dz = offset(k)
            packed[k, 0] = piece(dx, dz, 1)
            packed[k, 1] = piece(dx, dz, 0)
            pltpu.make_async_remote_copy(
                src_ref=packed.at[k],
                dst_ref=held.at[core, pl.ds(0, 2), k],
                send_sem=plane_send,
                recv_sem=plane_recv.at[g],
                device_id=device(x + dx, y, z + dz, core),
                device_id_type=MESH,
            ).start()
            return carry

        return send

    for g, (low, size, _) in sorted(enumerate(GROUPS), key=lambda item: item[1][0]):
        lax.fori_loop(max(low, 1), low + size, sender(g), 0)

    def arrived(g):
        low, size, _ = GROUPS[g]
        low, size = max(low, 1), low + size - max(low, 1)
        where = held.at[core, pl.ds(0, 2), pl.ds(low, size)]
        return pltpu.make_async_remote_copy(
            src_ref=where, dst_ref=where, send_sem=plane_send, recv_sem=plane_recv.at[g], device_id=other, device_id_type=MESH
        )

    def over_y(g, dy):
        here = pl.ds(*GROUPS[g][:2])
        return pltpu.make_async_remote_copy(
            src_ref=held.at[core, 1 if dy == 2 else 0, here],
            dst_ref=held.at[core, 1 + dy, here],
            send_sem=y_send.at[dy - 1],
            recv_sem=y_recv.at[dy - 1, g],
            device_id=device(x, y + dy, z, core),
            device_id_type=MESH,
        )

    def over_chip(g):
        where = held.at[core, pl.ds(1, 4), pl.ds(*GROUPS[g][:2])]
        return pltpu.make_async_remote_copy(
            src_ref=where, dst_ref=where, send_sem=core_send, recv_sem=core_recv.at[g], device_id=other, device_id_type=MESH
        )

    def assemble(g):
        low, size, _ = GROUPS[g]

        def block(n, carry):
            i, k = n // size, low + n % size
            dx, dz = offset(k)
            pool, fsdp, _ = device(x + NX - dx, y + NY - i, z + NZ - dz, 0)
            start = pl.multiple_of((pool * count + fsdp) * (2 * rows), 2 * rows)
            parts = []
            for c in (0, 1):
                value = held[c, 1 + i, k].astype(jnp.float32)
                parts.append(jnp.concatenate([value[:rows], value[rows:]], axis=1))
            rollout[pl.ds(start, 2 * rows), :] = jnp.concatenate(parts, axis=0).astype(jnp.bfloat16)
            return carry

        lax.fori_loop(0, 4 * size, block, 0)

    def take_plane(g):
        arrived(g).wait_recv()
        for dy in (1, 2, 3):
            over_y(g, dy).start()

    def take_y(g):
        for dy in (1, 2, 3):
            over_y(g, dy).wait_recv()
        over_chip(g).start()

    def take_chip(g):
        over_chip(g).wait_recv()
        assemble(g)

    events = []
    for g, (_, _, when) in enumerate(GROUPS):
        events += [(when, take_plane, g), (when + Y_TIME, take_y, g), (when + Y_TIME + CHIP_TIME, take_chip, g)]
    for _, take, g in sorted(events, key=lambda event: event[0]):
        take(g)

    def drain(ref, sem):
        pltpu.make_async_remote_copy(
            src_ref=ref, dst_ref=ref, send_sem=sem, recv_sem=plane_recv.at[0], device_id=other, device_id_type=MESH
        ).wait_send()

    drain(packed.at[pl.ds(1, STEPS - 1)], plane_send)
    for dy in (1, 2, 3):
        drain(held.at[core, 1 if dy == 2 else 0], y_send.at[dy - 1])
    drain(held.at[core, pl.ds(1, 4)], core_send)


def write(*refs):
    count = (len(refs) - 1) // 2
    copies = [pltpu.make_async_copy(refs[i], refs[count + i], refs[-1].at[i]) for i in range(count)]
    for copy in copies:
        copy.start()
    for copy in copies:
        copy.wait()


def per_device(master, grad, first_moment, second_moment, matching):
    rows, width = master.shape
    count = matching.shape[0]
    cols = width // count
    total = 2 * count * 2 * rows
    hbm = pl.BlockSpec(memory_space=pltpu.HBM)
    pin = functools.partial(pltpu.with_memory_space_constraint, memory_space=pltpu.HBM)
    vmem = pl.BlockSpec(memory_space=pltpu.VMEM)
    dma = pltpu.SemaphoreType.DMA
    results = pl.pallas_call(
        kernel,
        out_shape=[pltpu.VMEM((rows, width), jnp.float32)] * 3 + [pltpu.VMEM((total, cols), jnp.bfloat16)],
        in_specs=[hbm] * 5,
        out_specs=[vmem] * 4,
        scratch_shapes=[
            pltpu.VMEM((rows, width), jnp.float32),
            pltpu.VMEM((rows, width), jnp.bfloat16),
            pltpu.VMEM((rows, width), jnp.float32),
            pltpu.VMEM((rows, width), jnp.float32),
            pltpu.VMEM((count, 2 * rows, cols // 2), jnp.bfloat16),
            pltpu.VMEM((1, count), jnp.int32),
            pltpu.VMEM((1, count), jnp.int32),
            pltpu.SMEM((1, count), jnp.int32),
            pltpu.VMEM((STEPS, 2, 2 * rows, cols // 2), jnp.bfloat16),
            pltpu.VMEM((2, 5, STEPS, 2 * rows, cols // 2), jnp.bfloat16),
            dma((4, CHUNKS)),
            dma,
            dma,
            dma((len(GROUPS),)),
            dma((3,)),
            dma((3, len(GROUPS))),
            dma,
            dma((len(GROUPS),)),
        ],
        compiler_params=pltpu.CompilerParams(collective_id=0, has_side_effects=True, vmem_limit_bytes=20 << 20),
    )(*map(pin, (master, grad, first_moment, second_moment, matching.reshape(1, count))))
    new_master, new_first, new_second, rollout = pl.pallas_call(
        write,
        out_shape=[jax.ShapeDtypeStruct(r.shape, r.dtype) for r in results],
        in_specs=[vmem] * 4,
        out_specs=[hbm] * 4,
        scratch_shapes=[dma((4,))],
        compiler_params=pltpu.CompilerParams(vmem_limit_bytes=4 << 20),
    )(*(pltpu.with_memory_space_constraint(r, pltpu.VMEM) for r in results))
    return new_master, new_first, new_second, rollout.reshape(1, total, cols)


def solution(mesh):
    rows = P(("pool", "fsdp", "rep"), None)
    return jax.shard_map(
        per_device,
        mesh=mesh,
        in_specs=(rows, rows, rows, rows, P()),
        out_specs=(rows, rows, rows, P("fsdp", None, None)),
        check_vma=False,
    )
```

```python
import functools

import jax
import jax.numpy as jnp
from jax import lax
from jax.experimental import pallas as pl
from jax.experimental.pallas import tpu as pltpu
from jax.sharding import PartitionSpec as P

MESH = pl.DeviceIdType.MESH
beta_one = 0.9
beta_two = 0.95
learn_rate = 0.05
decay_rate = 0.1
epsilon = 1e-08
bias_one = 1.0 - 0.9**10
bias_two = 1.0 - 0.95**10

NX, NY, NZ = 4, 4, 8
STEPS = NX * NZ
GROUPS = tuple((NX * j, NX) for j in range(NZ))
ORDER = (
    (3.0, 0, None), (6.0, 1, (True, 1)), (6.5, 2, None), (9.0, 3, (True, 2)), (10.0, 4, None), (11.5, 1, (False, 1)),
    (13.0, 5, (True, 3)), (14.0, 6, None), (15.0, 3, (False, 2)), (17.0, 5, (False, 3)), (18.0, 7, None),
)
Y_TIME, CHIP_TIME = 6.0, 4.0
CHUNKS = 8


def place():
    pool, fsdp, core = lax.axis_index("pool"), lax.axis_index("fsdp"), lax.axis_index("rep")
    return fsdp % NX, pool * 2 + (fsdp // NX) % 2, fsdp // (2 * NX), core


def device(x, y, z, core):
    x, y, z, core = (x + NX) % NX, (y + NY) % NY, (z + NZ) % NZ, core % 2
    return (y // 2, z * (2 * NX) + (y % 2) * NX + x, core)


def offset(k):
    j = k // NX
    return k % NX, ((j + 1) // 2) * (2 * (j % 2) - 1)


def adamw(master, grad, first, second):
    gradient = grad.astype(jnp.float32)
    new_first = beta_one * first + (1.0 - beta_one) * gradient
    new_second = beta_two * second + (1.0 - beta_two) * gradient * gradient
    step = new_first * (learn_rate / bias_one)
    new_master = master * (1.0 - learn_rate * decay_rate) - step / (jnp.sqrt(new_second * (1.0 / bias_two)) + epsilon)
    return new_master, new_first, new_second


def kernel(
    master_hbm, grad_hbm, first_hbm, second_hbm, matching_hbm,
    new_master, new_first, new_second, rollout,
    master, grad, first, second, weights, matching, row, ranks, packed, held,
    in_sem, rank_sem, plane_send, plane_recv, y_send, y_recv, core_send, core_recv, down, up,
):
    rows, width = master.shape
    count = matching_hbm.shape[1]
    cols = width // count
    half = cols // 2
    x, y, z, core = place()
    other = device(x, y, z, core + 1)

    matching_load = pltpu.make_async_copy(matching_hbm, matching, rank_sem)
    matching_load.start()
    grad_load = pltpu.make_async_copy(grad_hbm, grad, in_sem.at[0, 0])
    grad_load.start()

    def load(t, i):
        where = pl.ds(t * (width // CHUNKS), width // CHUNKS)
        src, dst = ((master_hbm, master), (first_hbm, first), (second_hbm, second))[i]
        return pltpu.make_async_copy(src.at[:, where], dst.at[:, where], in_sem.at[1 + i, t])

    for t in range(CHUNKS):
        for i in range(3):
            load(t, i).start()

    barrier = pltpu.get_barrier_semaphore()

    def greet(dx, dy, dz, dc):
        pl.semaphore_signal(barrier, inc=1, device_id=device(x + dx, y + dy, z + dz, core + dc), device_id_type=MESH)

    for n in (1, 2, 3):
        greet(n, 0, 0, 0)
        greet(0, n, 0, 0)
    greet(0, 0, 0, 1)
    greet(0, 0, -1, 0)

    def tell(sem, j, dz):
        pl.semaphore_signal(sem.at[j], inc=1, device_id=device(x, y, z + dz, core), device_id_type=MESH)

    def enter():
        pl.semaphore_wait(barrier, 8)
        tell(down, 0, 1)

    def hear_down(j):
        pl.semaphore_wait(down.at[j - 1], 1)
        tell(up, j - 1, -j)
        if j < 3:
            tell(down, j, 1)
        elif j == 3:
            pl.when((z >= 3) & (z < NZ - 1))(lambda: tell(down, 3, 1))

    def hear_up(j):
        pl.semaphore_wait(up.at[j - 1], 1)

    matching_load.wait()
    lane = lax.broadcasted_iota(jnp.int32, (count, count), 1)
    sub = lax.broadcasted_iota(jnp.int32, (count, count), 0)
    hit = jnp.where(matching[...] == sub, lane, 0)
    column = jnp.max(hit, axis=1, keepdims=True)
    row[...] = jnp.sum(jnp.where(lane == sub, column, 0), axis=0, keepdims=True)
    to_scalar = pltpu.make_async_copy(row, ranks, rank_sem)
    to_scalar.start()
    to_scalar.wait()
    grad_load.wait()
    for t in range(CHUNKS):
        for i in range(3):
            load(t, i).wait()

        def block(n, carry):
            where = pl.ds(pl.multiple_of(n * cols, cols), cols)
            value, new_first[:, where], new_second[:, where] = adamw(
                master[:, where], grad[:, where], first[:, where], second[:, where]
            )
            new_master[:, where] = value
            weights[n] = jnp.concatenate([value[:, :half], value[:, half:]], axis=0).astype(jnp.bfloat16)
            return carry

        lax.fori_loop(t * (count // CHUNKS), (t + 1) * (count // CHUNKS), block, 0)
        if t == 3:
            enter()
        elif t > 3:
            pl.when(z >= t - 3)(functools.partial(hear_down, t - 3))

    def piece(dx, dz, parity):
        host = ((z + NZ + dz) % NZ) * (2 * NX) + ((y + parity) % 2) * NX + (x + dx) % NX
        return weights[ranks[0, host]]

    held[core, 0, 0] = piece(0, 0, 1)
    held[core, 1, 0] = piece(0, 0, 0)

    def sender(g):
        def send(k, carry):
            dx, dz = offset(k)
            packed[k, 0] = piece(dx, dz, 1)
            packed[k, 1] = piece(dx, dz, 0)
            pltpu.make_async_remote_copy(
                src_ref=packed.at[k],
                dst_ref=held.at[core, pl.ds(0, 2), k],
                send_sem=plane_send,
                recv_sem=plane_recv.at[g],
                device_id=device(x + dx, y, z + dz, core),
                device_id_type=MESH,
            ).start()
            return carry

        return send

    def send_group(g):
        low, size = GROUPS[g]
        lax.fori_loop(max(low, 1), low + size, sender(g), 0)

    def send_up(j):
        hear_up(j)
        send_group(2 * j - 1)

    def send_down(j):
        send_group(2 * j)

    def send_down_late(j):
        hear_down(j)
        send_down(j)

    send_group(0)
    pl.when(z >= 1)(lambda: send_down(1))
    send_up(1)
    pl.when(z >= 2)(lambda: send_down(2))
    send_up(2)
    pl.when(z < 1)(lambda: send_down_late(1))
    pl.when(z >= 3)(lambda: send_down(3))
    pl.when(z < 2)(lambda: send_down_late(2))
    send_up(3)
    pl.when(z < 3)(lambda: send_down_late(3))
    pl.when(z < 4)(lambda: hear_up(4))
    send_group(7)

    def arrived(g):
        low, size = GROUPS[g]
        low, size = max(low, 1), low + size - max(low, 1)
        where = held.at[core, pl.ds(0, 2), pl.ds(low, size)]
        return pltpu.make_async_remote_copy(
            src_ref=where, dst_ref=where, send_sem=plane_send, recv_sem=plane_recv.at[g], device_id=other, device_id_type=MESH
        )

    def over_y(g, dy):
        here = pl.ds(*GROUPS[g])
        return pltpu.make_async_remote_copy(
            src_ref=held.at[core, 1 if dy == 2 else 0, here],
            dst_ref=held.at[core, 1 + dy, here],
            send_sem=y_send.at[dy - 1],
            recv_sem=y_recv.at[dy - 1, g],
            device_id=device(x, y + dy, z, core),
            device_id_type=MESH,
        )

    def over_chip(g):
        where = held.at[core, pl.ds(1, 4), pl.ds(*GROUPS[g])]
        return pltpu.make_async_remote_copy(
            src_ref=where, dst_ref=where, send_sem=core_send, recv_sem=core_recv.at[g], device_id=other, device_id_type=MESH
        )

    def assemble(g):
        low, size = GROUPS[g]

        def block(n, carry):
            i, k = n // size, low + n % size
            dx, dz = offset(k)
            pool, fsdp, _ = device(x + NX - dx, y + NY - i, z + NZ - dz, 0)
            start = pl.multiple_of((pool * count + fsdp) * (2 * rows), 2 * rows)
            parts = []
            for c in (0, 1):
                value = held[c, 1 + i, k].astype(jnp.float32)
                parts.append(jnp.concatenate([value[:rows], value[rows:]], axis=1))
            rollout[pl.ds(start, 2 * rows), :] = jnp.concatenate(parts, axis=0).astype(jnp.bfloat16)
            return carry

        lax.fori_loop(0, 4 * size, block, 0)

    def take_plane(g):
        arrived(g).wait_recv()
        for dy in (1, 2, 3):
            over_y(g, dy).start()

    def take_y(g):
        for dy in (1, 2, 3):
            over_y(g, dy).wait_recv()
        over_chip(g).start()

    def take_chip(g):
        over_chip(g).wait_recv()
        assemble(g)

    events = []
    for when, g, only in ORDER:
        events += [(when, take_plane, g, only), (when + Y_TIME, take_y, g, only), (when + Y_TIME + CHIP_TIME, take_chip, g, only)]
    for _, take, g, only in sorted(events, key=lambda event: event[0]):
        if only is None:
            take(g)
        else:
            pl.when(z >= only[1] if only[0] else z < only[1])(functools.partial(take, g))

    def drain(ref, sem):
        pltpu.make_async_remote_copy(
            src_ref=ref, dst_ref=ref, send_sem=sem, recv_sem=plane_recv.at[0], device_id=other, device_id_type=MESH
        ).wait_send()

    drain(packed.at[pl.ds(1, STEPS - 1)], plane_send)
    for dy in (1, 2, 3):
        drain(held.at[core, 1 if dy == 2 else 0], y_send.at[dy - 1])
    drain(held.at[core, pl.ds(1, 4)], core_send)


def write(*refs):
    count = (len(refs) - 1) // 2
    copies = [pltpu.make_async_copy(refs[i], refs[count + i], refs[-1].at[i]) for i in range(count)]
    for copy in copies:
        copy.start()
    for copy in copies:
        copy.wait()


def per_device(master, grad, first_moment, second_moment, matching):
    rows, width = master.shape
    count = matching.shape[0]
    cols = width // count
    total = 2 * count * 2 * rows
    hbm = pl.BlockSpec(memory_space=pltpu.HBM)
    pin = functools.partial(pltpu.with_memory_space_constraint, memory_space=pltpu.HBM)
    vmem = pl.BlockSpec(memory_space=pltpu.VMEM)
    dma = pltpu.SemaphoreType.DMA
    results = pl.pallas_call(
        kernel,
        out_shape=[pltpu.VMEM((rows, width), jnp.float32)] * 3 + [pltpu.VMEM((total, cols), jnp.bfloat16)],
        in_specs=[hbm] * 5,
        out_specs=[vmem] * 4,
        scratch_shapes=[
            pltpu.VMEM((rows, width), jnp.float32),
            pltpu.VMEM((rows, width), jnp.bfloat16),
            pltpu.VMEM((rows, width), jnp.float32),
            pltpu.VMEM((rows, width), jnp.float32),
            pltpu.VMEM((count, 2 * rows, cols // 2), jnp.bfloat16),
            pltpu.VMEM((1, count), jnp.int32),
            pltpu.VMEM((1, count), jnp.int32),
            pltpu.SMEM((1, count), jnp.int32),
            pltpu.VMEM((STEPS, 2, 2 * rows, cols // 2), jnp.bfloat16),
            pltpu.VMEM((2, 5, STEPS, 2 * rows, cols // 2), jnp.bfloat16),
            dma((4, CHUNKS)),
            dma,
            dma,
            dma((len(GROUPS),)),
            dma((3,)),
            dma((3, len(GROUPS))),
            dma,
            dma((len(GROUPS),)),
            pltpu.SemaphoreType.REGULAR((4,)),
            pltpu.SemaphoreType.REGULAR((4,)),
        ],
        compiler_params=pltpu.CompilerParams(collective_id=0, has_side_effects=True, vmem_limit_bytes=20 << 20),
    )(*map(pin, (master, grad, first_moment, second_moment, matching.reshape(1, count))))
    new_master, new_first, new_second, rollout = pl.pallas_call(
        write,
        out_shape=[jax.ShapeDtypeStruct(r.shape, r.dtype) for r in results],
        in_specs=[vmem] * 4,
        out_specs=[hbm] * 4,
        scratch_shapes=[dma((4,))],
        compiler_params=pltpu.CompilerParams(vmem_limit_bytes=4 << 20),
    )(*(pltpu.with_memory_space_constraint(r, pltpu.VMEM) for r in results))
    return new_master, new_first, new_second, rollout.reshape(1, total, cols)


def solution(mesh):
    rows = P(("pool", "fsdp", "rep"), None)
    return jax.shard_map(
        per_device,
        mesh=mesh,
        in_specs=(rows, rows, rows, rows, P()),
        out_specs=(rows, rows, rows, P("fsdp", None, None)),
        check_vma=False,
    )
```

```python
import functools

import jax
import jax.numpy as jnp
from jax import lax
from jax.experimental import pallas as pl
from jax.experimental.pallas import tpu as pltpu
from jax.sharding import PartitionSpec as P

MESH = pl.DeviceIdType.MESH
beta_one = 0.9
beta_two = 0.95
learn_rate = 0.05
decay_rate = 0.1
epsilon = 1e-08
bias_one = 1.0 - 0.9**10
bias_two = 1.0 - 0.95**10

NX, NY, NZ = 4, 4, 8
STEPS = NX * NZ
CHUNKS = 4
UNROLL = 8

GROUPS = tuple((NX * (j + 1) + (0, 1, 3)[n], (1, 2, 1)[n]) for j in range(NZ - 1) for n in range(3))
NEAR = len(GROUPS)
TIMES = (
    (1, (4.0, 5.0, 5.8), lambda z: z >= 1), (2, (4.1, 5.1, 5.9), None), (3, (6.5, 7.5, 8.2), lambda z: z >= 2), (4, (7.0, 8.0, 9.0), None),
    (1, (9.5, 10.0, 10.5), lambda z: z < 1), (5, (10.5, 11.5, 12.5), lambda z: z >= 3), (6, (11.0, 12.0, 13.0), None),
    (3, (13.0, 13.5, 14.0), lambda z: z < 2), (5, (15.0, 15.5, 16.0), lambda z: z < 3), (7, (15.1, 16.1, 17.0), None),
)
SENDS = (
    (0.05, 2, lambda z: z >= 1, True, True), (0.2, 4, lambda z: z >= 2, True, True), (0.3, 6, lambda z: z >= 3, True, True),
    (1.2, 1, None, True, True), (1.3, 7, lambda z: z >= 4, True, False), (1.8, 3, None, True, True), (3.2, 2, lambda z: z < 1, True, True),
    (3.3, 5, None, True, True), (3.4, 4, lambda z: z < 2, True, True), (4.4, 6, lambda z: z < 3, True, True),
    (4.5, 7, lambda z: z < 4, True, False), (4.6, 7, None, False, True),
)
Y_TIME = 6.0

def place():
    pool, fsdp, core = lax.axis_index("pool"), lax.axis_index("fsdp"), lax.axis_index("rep")
    return fsdp % NX, pool * 2 + (fsdp // NX) % 2, fsdp // (2 * NX), core


def device(x, y, z, core):
    x, y, z, core = (x + NX) % NX, (y + NY) % NY, (z + NZ) % NZ, core % 2
    return (y // 2, z * (2 * NX) + (y % 2) * NX + x, core)


def offset(k):
    i, j = k % NX, k // NX
    return i + (i // 2) * (1 - 2 * (i % 2)), ((j + 1) // 2) * (2 * (j % 2) - 1)


def adamw(master, grad, first, second):
    gradient = grad.astype(jnp.float32)
    new_first = beta_one * first + (1.0 - beta_one) * gradient
    new_second = beta_two * second + (1.0 - beta_two) * gradient * gradient
    scaled = new_second * (1.0 / bias_two)
    root = scaled * lax.rsqrt(scaled)
    step = new_first * (learn_rate / bias_one)
    new_master = master * (1.0 - learn_rate * decay_rate) - step / (root + epsilon)
    return new_master, new_first, new_second


def kernel(
    master_hbm, grad_hbm, first_hbm, second_hbm, matching_hbm,
    new_master, new_first, new_second, held,
    master, grad, first, second, weights, matching, row, ranks, packed,
    in_sem, rank_sem, plane_send, plane_recv, y_send, y_recv, core_send, core_recv, near_send, near_recv, down, up,
):
    rows, width = master.shape
    count = matching_hbm.shape[1]
    cols = width // count
    half = cols // 2
    x, y, z, core = place()
    other = device(x, y, z, core + 1)

    matching_load = pltpu.make_async_copy(matching_hbm, matching, rank_sem)
    matching_load.start()
    grad_load = pltpu.make_async_copy(grad_hbm, grad, in_sem.at[0, 0])
    grad_load.start()

    def load(t, i):
        where = pl.ds(t * (width // CHUNKS), width // CHUNKS)
        src, dst = ((master_hbm, master), (first_hbm, first), (second_hbm, second))[i]
        return pltpu.make_async_copy(src.at[:, where], dst.at[:, where], in_sem.at[1 + i, t])

    for t in range(CHUNKS):
        for i in range(3):
            load(t, i).start()

    barrier = pltpu.get_barrier_semaphore()

    def greet(dx, dy, dz, dc):
        pl.semaphore_signal(barrier, inc=1, device_id=device(x + dx, y + dy, z + dz, core + dc), device_id_type=MESH)

    def greet_near(n, carry):
        greet(n % NX, n // NX, 0, 0)
        return carry

    greet(0, 0, 0, 1)
    greet(0, 0, -1, 0)
    lax.fori_loop(1, NX * NY, greet_near, 0)

    def tell(sem, j, dz):
        pl.semaphore_signal(sem.at[j], inc=1, device_id=device(x, y, z + dz, core), device_id_type=MESH)

    def enter():
        pl.semaphore_wait(barrier, 2 + NX * NY - 1)
        tell(down, 0, 1)

    def hear_down(j):
        pl.semaphore_wait(down.at[j - 1], 1)
        tell(up, j - 1, -j)
        if j < 3:
            tell(down, j, 1)
        elif j == 3:
            pl.when((z >= 3) & (z < NZ - 1))(lambda: tell(down, 3, 1))

    def hear_up(j):
        pl.semaphore_wait(up.at[j - 1], 1)

    to_scalar = pltpu.make_async_copy(row, ranks, rank_sem)

    def look_up():
        matching_load.wait()
        lane = lax.broadcasted_iota(jnp.int32, (count, count), 1)
        sub = lax.broadcasted_iota(jnp.int32, (count, count), 0)
        hit = jnp.where(matching[...] == sub, lane, 0)
        column = jnp.max(hit, axis=1, keepdims=True)
        row[...] = jnp.sum(jnp.where(lane == sub, column, 0), axis=0, keepdims=True)
        to_scalar.start()

    grad_load.wait()
    for t in range(CHUNKS):
        for i in range(3):
            load(t, i).wait()

        def blocks(n, carry):
            for u in range(UNROLL):
                where = pl.ds(pl.multiple_of((n * UNROLL + u) * cols, cols), cols)
                value, new_first[:, where], new_second[:, where] = adamw(
                    master[:, where], grad[:, where], first[:, where], second[:, where]
                )
                new_master[:, where] = value
                value = jnp.concatenate([value[:, :half], value[:, half:]], axis=0)
                weights[n * UNROLL + u] = value.astype(jnp.bfloat16)
            return carry

        per = count // CHUNKS // UNROLL
        lax.fori_loop(t * per, (t + 1) * per, blocks, 0)
        if t == 1:
            look_up()
        elif t == 3:
            enter()
    to_scalar.wait()

    across = [lax.rem(x + offset(i)[0], NX) for i in range(NX)]
    lows = (lax.rem(y + 1, 2) * NX, lax.rem(y, 2) * NX)
    near_hosts = [(across[i] + lows[0], across[i] + lows[1]) for i in range(NX)]

    def pack(j, carry):
        plane = lax.rem(z + NZ + offset(j * NX)[1], NZ) * (2 * NX)
        for i in range(NX):
            for own in (0, 1):
                packed[j * NX + i, own] = weights[ranks[0, plane + near_hosts[i][own]]]
        return carry

    lax.fori_loop(0, NZ, pack, 0)
    held[core, 1, 0] = packed[0, 1]

    for k in range(NX):
        for dy in (2, 1, 3, 0) if k else (2, 1, 3):
            pltpu.make_async_remote_copy(
                src_ref=packed.at[k, (dy + 1) % 2],
                dst_ref=held.at[core, 1 + dy, k],
                send_sem=y_send.at[dy - 1] if dy else near_send,
                recv_sem=y_recv.at[dy - 1, NEAR] if dy else near_recv,
                device_id=device(x + offset(k)[0], y + dy, z, core),
                device_id_type=MESH,
            ).start()

    def send_plane(j):
        plane = lax.rem(z + NZ + offset(j * NX)[1], NZ) * (2 * NX)
        for i in range(NX):
            k = j * NX + i
            pltpu.make_async_remote_copy(
                src_ref=packed.at[k],
                dst_ref=held.at[core, pl.ds(0, 2), k],
                send_sem=plane_send,
                recv_sem=plane_recv.at[(j - 1) * 3 + (0, 1, 1, 2)[i]],
                device_id=(y // 2, plane + near_hosts[i][1], core),
                device_id_type=MESH,
            ).start()

    def hear(j, late):
        if j == 7 and late:
            hear_up(4)
        elif j % 2 and j < 7:
            hear_up((j + 1) // 2)
        else:
            hear_down((j + 1) // 2)

    lines = {dy: device(x, y + dy, z, core) for dy in (1, 2, 3)}

    def arrived(g):
        where = held.at[core, pl.ds(0, 2), pl.ds(*GROUPS[g])]
        return pltpu.make_async_remote_copy(
            src_ref=where, dst_ref=where, send_sem=plane_send, recv_sem=plane_recv.at[g], device_id=other, device_id_type=MESH
        )

    def near(sem):
        where = held.at[core, 1, pl.ds(1, NX - 1)]
        return pltpu.make_async_remote_copy(
            src_ref=where, dst_ref=where, send_sem=near_send, recv_sem=sem, device_id=other, device_id_type=MESH
        )

    def over_y(g, dy):
        here = pl.ds(0, NX) if g == NEAR else pl.ds(*GROUPS[g])
        return pltpu.make_async_remote_copy(
            src_ref=held.at[core, 1 if dy == 2 else 0, here],
            dst_ref=held.at[core, 1 + dy, here],
            send_sem=y_send.at[dy - 1],
            recv_sem=y_recv.at[dy - 1, g],
            device_id=lines[dy],
            device_id_type=MESH,
        )

    def over_chip(n):
        where = held.at[core, pl.ds(1, 4), pl.ds(n * NX, NX)]
        return pltpu.make_async_remote_copy(
            src_ref=where, dst_ref=where, send_sem=core_send, recv_sem=core_recv.at[n], device_id=other, device_id_type=MESH
        )

    def take_plane(g):
        arrived(g).wait_recv()
        for dy in (1, 2, 3):
            over_y(g, dy).start()

    def take_y(g):
        for dy in (1, 2, 3):
            over_y(g, dy).wait_recv()
        if g == NEAR:
            near(near_recv).wait_recv()
            over_chip(0).start()
        elif g % 3 == 2:
            over_chip(g // 3 + 1).start()

    events = [(5.0, None, functools.partial(take_y, NEAR))]
    for when, j, only, listen, go in SENDS:
        if listen:
            events.append((when, only, functools.partial(hear, j, when > 4)))
        if go:
            events.append((when + 0.001, only, functools.partial(send_plane, j)))
    for j, times, only in TIMES:
        for n, when in enumerate(times):
            g = (j - 1) * 3 + n
            events.append((when, only, functools.partial(take_plane, g)))
            events.append((when + Y_TIME, only, functools.partial(take_y, g)))
    for _, only, take in sorted(events, key=lambda event: event[0]):
        if only is None:
            take()
        else:
            pl.when(only(z))(take)

    for n in range(NZ):
        over_chip(n).wait_recv()

    def drain(ref, sem):
        pltpu.make_async_remote_copy(
            src_ref=ref, dst_ref=ref, send_sem=sem, recv_sem=plane_recv.at[0], device_id=other, device_id_type=MESH
        ).wait_send()

    near(near_recv).wait_send()
    drain(packed.at[pl.ds(NX, STEPS - NX)], plane_send)
    for dy in (1, 2, 3):
        drain(held.at[core, 1 if dy == 2 else 0], y_send.at[dy - 1])
    drain(held.at[core, pl.ds(1, 4)], core_send)


def write(new_master, new_first, new_second, held, out_master, out_first, out_second, out_rollout, rollout, whole_sem, part_sem):
    x, y, z, _ = place()
    rows = new_master.shape[0]
    count = NX * 2 * NZ
    wholes = [
        pltpu.make_async_copy(src, dst, whole_sem.at[i])
        for i, (src, dst) in enumerate(((new_master, out_master), (new_first, out_first), (new_second, out_second)))
    ]

    def block(i, k):
        dx, dz = offset(k)
        pool, fsdp, _ = device(x + NX - dx, y + NY - i, z + NZ - dz, 0)
        start = pl.multiple_of((pool * count + fsdp) * (2 * rows), 2 * rows)
        parts = []
        for c in (0, 1):
            value = held[c, 1 + i, k].astype(jnp.float32)
            parts.append(jnp.concatenate([value[:rows], value[rows:]], axis=1))
        rollout[pl.ds(start, 2 * rows), :] = jnp.concatenate(parts, axis=0).astype(jnp.bfloat16)

    def part(j, pool):
        _, dz = offset(j * NX)
        size = NX * 2 * 2 * rows
        where = pl.ds(pl.multiple_of((pool * NZ + (z + NZ - dz) % NZ) * size, size), size)
        return pltpu.make_async_copy(rollout.at[where], out_rollout.at[where], part_sem.at[j, pool])

    for j in range(NZ):

        def blocks(n, carry):
            for i in range(NY):
                block(i, j * NX + n)
            return carry

        lax.fori_loop(0, NX, blocks, 0)
        for pool in (0, 1):
            part(j, pool).start()
        if j < len(wholes):
            wholes[j].start()
    for copy in wholes:
        copy.wait()
    for j in range(NZ):
        for pool in (0, 1):
            part(j, pool).wait()


def per_device(master, grad, first_moment, second_moment, matching):
    rows, width = master.shape
    count = matching.shape[0]
    cols = width // count
    total = 2 * count * 2 * rows
    hbm = pl.BlockSpec(memory_space=pltpu.HBM)
    pin = functools.partial(pltpu.with_memory_space_constraint, memory_space=pltpu.HBM)
    vmem = pl.BlockSpec(memory_space=pltpu.VMEM)
    dma = pltpu.SemaphoreType.DMA
    results = pl.pallas_call(
        kernel,
        out_shape=[pltpu.VMEM((rows, width), jnp.float32)] * 3 + [pltpu.VMEM((2, 1 + NY, STEPS, 2 * rows, cols // 2), jnp.bfloat16)],
        in_specs=[hbm] * 5,
        out_specs=[vmem] * 4,
        scratch_shapes=[
            pltpu.VMEM((rows, width), jnp.float32),
            pltpu.VMEM((rows, width), jnp.bfloat16),
            pltpu.VMEM((rows, width), jnp.float32),
            pltpu.VMEM((rows, width), jnp.float32),
            pltpu.VMEM((count, 2 * rows, cols // 2), jnp.bfloat16),
            pltpu.VMEM((1, count), jnp.int32),
            pltpu.VMEM((1, count), jnp.int32),
            pltpu.SMEM((1, count), jnp.int32),
            pltpu.VMEM((STEPS, 2, 2 * rows, cols // 2), jnp.bfloat16),
            dma((4, CHUNKS)),
            dma,
            dma,
            dma((len(GROUPS),)),
            dma((3,)),
            dma((3, len(GROUPS) + 1)),
            dma,
            dma((NZ,)),
            dma,
            dma,
            pltpu.SemaphoreType.REGULAR((4,)),
            pltpu.SemaphoreType.REGULAR((4,)),
        ],
        compiler_params=pltpu.CompilerParams(collective_id=0, has_side_effects=True, vmem_limit_bytes=20 << 20),
    )(*map(pin, (master, grad, first_moment, second_moment, matching.reshape(1, count))))
    new_master, new_first, new_second, rollout = pl.pallas_call(
        write,
        out_shape=[jax.ShapeDtypeStruct((rows, width), jnp.float32)] * 3 + [jax.ShapeDtypeStruct((total, cols), jnp.bfloat16)],
        in_specs=[vmem] * 4,
        out_specs=[hbm] * 4,
        scratch_shapes=[pltpu.VMEM((total, cols), jnp.bfloat16), dma((3,)), dma((NZ, 2))],
        compiler_params=pltpu.CompilerParams(vmem_limit_bytes=8 << 20),
    )(*(pltpu.with_memory_space_constraint(r, pltpu.VMEM) for r in results))
    return new_master, new_first, new_second, rollout.reshape(1, total, cols)


def solution(mesh):
    rows = P(("pool", "fsdp", "rep"), None)
    return jax.shard_map(
        per_device,
        mesh=mesh,
        in_specs=(rows, rows, rows, rows, P()),
        out_specs=(rows, rows, rows, P("fsdp", None, None)),
        check_vma=False,
    )
```

```python
import functools

import jax
import jax.numpy as jnp
from jax import lax
from jax.experimental import pallas as pl
from jax.experimental.pallas import tpu as pltpu
from jax.sharding import PartitionSpec as P

MESH = pl.DeviceIdType.MESH
beta_one = 0.9
beta_two = 0.95
learn_rate = 0.05
decay_rate = 0.1
epsilon = 1e-08
bias_one = 1.0 - 0.9**10
bias_two = 1.0 - 0.95**10

NX, NY, NZ = 4, 4, 8
STEPS = NX * NZ
CHUNKS = 4
UNROLL = 8

GROUPS = tuple((NX * (j + 1) + (0, 1, 3)[n], (1, 2, 1)[n]) for j in range(NZ - 1) for n in range(3))
NEAR = len(GROUPS)
TIMES = (
    (1, (4.0, 5.0, 5.8), lambda z: z >= 1), (2, (4.1, 5.1, 5.9), None), (3, (6.5, 7.5, 8.2), lambda z: z >= 2), (4, (7.0, 8.0, 9.0), None),
    (1, (9.5, 10.0, 10.5), lambda z: z < 1), (5, (10.5, 11.5, 12.5), lambda z: z >= 3), (6, (11.0, 12.0, 13.0), None),
    (3, (13.0, 13.5, 14.0), lambda z: z < 2), (5, (15.0, 15.5, 16.0), lambda z: z < 3), (7, (15.1, 16.1, 17.0), None),
)
SENDS = (
    (0.05, 2, lambda z: z >= 1, True, True), (0.2, 4, lambda z: z >= 2, True, True), (0.3, 6, lambda z: z >= 3, True, True),
    (1.2, 1, None, True, True), (1.3, 7, lambda z: z >= 4, True, False), (1.8, 3, None, True, True), (3.2, 2, lambda z: z < 1, True, True),
    (3.3, 5, None, True, True), (3.4, 4, lambda z: z < 2, True, True), (4.4, 6, lambda z: z < 3, True, True),
    (4.5, 7, lambda z: z < 4, True, False), (4.6, 7, None, False, True),
)
Y_TIME = 6.0

def place():
    pool, fsdp, core = lax.axis_index("pool"), lax.axis_index("fsdp"), lax.axis_index("rep")
    return fsdp % NX, pool * 2 + (fsdp // NX) % 2, fsdp // (2 * NX), core


def device(x, y, z, core):
    x, y, z, core = (x + NX) % NX, (y + NY) % NY, (z + NZ) % NZ, core % 2
    return (y // 2, z * (2 * NX) + (y % 2) * NX + x, core)


def offset(k):
    i, j = k % NX, k // NX
    return i + (i // 2) * (1 - 2 * (i % 2)), ((j + 1) // 2) * (2 * (j % 2) - 1)


def adamw(master, grad, first, second):
    gradient = grad.astype(jnp.float32)
    new_first = beta_one * first + (1.0 - beta_one) * gradient
    new_second = beta_two * second + (1.0 - beta_two) * gradient * gradient
    scaled = new_second * (1.0 / bias_two)
    root = scaled * lax.rsqrt(scaled)
    step = new_first * (learn_rate / bias_one)
    new_master = master * (1.0 - learn_rate * decay_rate) - step / (root + epsilon)
    return new_master, new_first, new_second


def kernel(
    master_hbm, grad_hbm, first_hbm, second_hbm, matching_hbm,
    new_master, new_first, new_second, held,
    master, grad, first, second, weights, matching, row, ranks, packed,
    in_sem, rank_sem, plane_send, plane_recv, y_send, y_recv, core_send, core_recv, near_send, near_recv, down, up,
):
    rows, width = master.shape
    count = matching_hbm.shape[1]
    cols = width // count
    half = cols // 2
    x, y, z, core = place()
    other = device(x, y, z, core + 1)

    matching_load = pltpu.make_async_copy(matching_hbm, matching, rank_sem)
    matching_load.start()
    grad_load = pltpu.make_async_copy(grad_hbm, grad, in_sem.at[0, 0])
    grad_load.start()

    def load(t, i):
        where = pl.ds(t * (width // CHUNKS), width // CHUNKS)
        src, dst = ((master_hbm, master), (first_hbm, first), (second_hbm, second))[i]
        return pltpu.make_async_copy(src.at[:, where], dst.at[:, where], in_sem.at[1 + i, t])

    for t in range(CHUNKS):
        for i in range(3):
            load(t, i).start()

    barrier = pltpu.get_barrier_semaphore()

    def greet(dx, dy, dz, dc):
        pl.semaphore_signal(barrier, inc=1, device_id=device(x + dx, y + dy, z + dz, core + dc), device_id_type=MESH)

    def greet_near(n, carry):
        greet(n % NX, n // NX, 0, 0)
        return carry

    greet(0, 0, 0, 1)
    greet(0, 0, -1, 0)
    lax.fori_loop(1, NX * NY, greet_near, 0)

    def tell(sem, j, dz):
        pl.semaphore_signal(sem.at[j], inc=1, device_id=device(x, y, z + dz, core), device_id_type=MESH)

    def enter():
        pl.semaphore_wait(barrier, 2 + NX * NY - 1)
        tell(down, 0, 1)

    def hear_down(j):
        pl.semaphore_wait(down.at[j - 1], 1)
        tell(up, j - 1, -j)
        if j < 3:
            tell(down, j, 1)
        elif j == 3:
            pl.when((z >= 3) & (z < NZ - 1))(lambda: tell(down, 3, 1))

    def hear_up(j):
        pl.semaphore_wait(up.at[j - 1], 1)

    to_scalar = pltpu.make_async_copy(row, ranks, rank_sem)

    def look_up():
        matching_load.wait()
        lane = lax.broadcasted_iota(jnp.int32, (count, count), 1)
        sub = lax.broadcasted_iota(jnp.int32, (count, count), 0)
        hit = jnp.where(matching[...] == sub, lane, 0)
        column = jnp.max(hit, axis=1, keepdims=True)
        row[...] = jnp.sum(jnp.where(lane == sub, column, 0), axis=0, keepdims=True)
        to_scalar.start()

    grad_load.wait()
    for t in range(CHUNKS):
        for i in range(3):
            load(t, i).wait()

        def blocks(n, carry):
            for u in range(UNROLL):
                where = pl.ds(pl.multiple_of((n * UNROLL + u) * cols, cols), cols)
                value, new_first[:, where], new_second[:, where] = adamw(
                    master[:, where], grad[:, where], first[:, where], second[:, where]
                )
                new_master[:, where] = value
                value = jnp.concatenate([value[:, :half], value[:, half:]], axis=0)
                weights[n * UNROLL + u] = value.astype(jnp.bfloat16)
            return carry

        per = count // CHUNKS // UNROLL
        lax.fori_loop(t * per, (t + 1) * per, blocks, 0)
        if t == 1:
            look_up()
        elif t == 3:
            enter()
    to_scalar.wait()

    across = [lax.rem(x + offset(i)[0], NX) for i in range(NX)]
    lows = (lax.rem(y + 1, 2) * NX, lax.rem(y, 2) * NX)
    near_hosts = [(across[i] + lows[0], across[i] + lows[1]) for i in range(NX)]

    def pack(j, carry):
        plane = lax.rem(z + NZ + offset(j * NX)[1], NZ) * (2 * NX)
        for i in range(NX):
            for own in (0, 1):
                packed[j * NX + i, own] = weights[ranks[0, plane + near_hosts[i][own]]]
        return carry

    lax.fori_loop(0, NZ, pack, 0)
    held[core, 1, 0] = packed[0, 1]

    for k in range(NX):
        for dy in (2, 1, 3, 0) if k else (2, 1, 3):
            pltpu.make_async_remote_copy(
                src_ref=packed.at[k, (dy + 1) % 2],
                dst_ref=held.at[core, 1 + dy, k],
                send_sem=y_send.at[dy - 1] if dy else near_send,
                recv_sem=y_recv.at[dy - 1, NEAR] if dy else near_recv,
                device_id=device(x + offset(k)[0], y + dy, z, core),
                device_id_type=MESH,
            ).start()

    def send_plane(j):
        plane = lax.rem(z + NZ + offset(j * NX)[1], NZ) * (2 * NX)
        for i in range(NX):
            k = j * NX + i
            pltpu.make_async_remote_copy(
                src_ref=packed.at[k],
                dst_ref=held.at[core, pl.ds(0, 2), k],
                send_sem=plane_send,
                recv_sem=plane_recv.at[(j - 1) * 3 + (0, 1, 1, 2)[i]],
                device_id=(y // 2, plane + near_hosts[i][1], core),
                device_id_type=MESH,
            ).start()

    def hear(j, late):
        if j == 7 and late:
            hear_up(4)
        elif j % 2 and j < 7:
            hear_up((j + 1) // 2)
        else:
            hear_down((j + 1) // 2)

    lines = {dy: device(x, y + dy, z, core) for dy in (1, 2, 3)}

    def arrived(g):
        where = held.at[core, pl.ds(0, 2), pl.ds(*GROUPS[g])]
        return pltpu.make_async_remote_copy(
            src_ref=where, dst_ref=where, send_sem=plane_send, recv_sem=plane_recv.at[g], device_id=other, device_id_type=MESH
        )

    def near(sem):
        where = held.at[core, 1, pl.ds(1, NX - 1)]
        return pltpu.make_async_remote_copy(
            src_ref=where, dst_ref=where, send_sem=near_send, recv_sem=sem, device_id=other, device_id_type=MESH
        )

    def over_y(g, dy):
        here = pl.ds(0, NX) if g == NEAR else pl.ds(*GROUPS[g])
        return pltpu.make_async_remote_copy(
            src_ref=held.at[core, 1 if dy == 2 else 0, here],
            dst_ref=held.at[core, 1 + dy, here],
            send_sem=y_send.at[dy - 1],
            recv_sem=y_recv.at[dy - 1, g],
            device_id=lines[dy],
            device_id_type=MESH,
        )

    def over_chip(n):
        where = held.at[core, pl.ds(1, 4), pl.ds(n * NX, NX)]
        return pltpu.make_async_remote_copy(
            src_ref=where, dst_ref=where, send_sem=core_send, recv_sem=core_recv.at[n], device_id=other, device_id_type=MESH
        )

    def take_plane(g):
        arrived(g).wait_recv()
        for dy in (1, 2, 3):
            over_y(g, dy).start()

    def take_y(g):
        for dy in (1, 2, 3):
            over_y(g, dy).wait_recv()
        if g == NEAR:
            near(near_recv).wait_recv()
            over_chip(0).start()
        elif g % 3 == 2:
            over_chip(g // 3 + 1).start()

    events = [(5.0, None, functools.partial(take_y, NEAR))]
    for when, j, only, listen, go in SENDS:
        if listen:
            events.append((when, only, functools.partial(hear, j, when > 4)))
        if go:
            events.append((when + 0.001, only, functools.partial(send_plane, j)))
    for j, times, only in TIMES:
        for n, when in enumerate(times):
            g = (j - 1) * 3 + n
            events.append((when, only, functools.partial(take_plane, g)))
            events.append((when + Y_TIME, only, functools.partial(take_y, g)))
    for _, only, take in sorted(events, key=lambda event: event[0]):
        if only is None:
            take()
        else:
            pl.when(only(z))(take)

    for n in range(NZ):
        over_chip(n).wait_recv()

    def drain(ref, sem):
        pltpu.make_async_remote_copy(
            src_ref=ref, dst_ref=ref, send_sem=sem, recv_sem=plane_recv.at[0], device_id=other, device_id_type=MESH
        ).wait_send()

    near(near_recv).wait_send()
    drain(packed.at[pl.ds(NX, STEPS - NX)], plane_send)
    for dy in (1, 2, 3):
        drain(held.at[core, 1 if dy == 2 else 0], y_send.at[dy - 1])
    drain(held.at[core, pl.ds(1, 4)], core_send)


def write(new_master, new_first, new_second, held, out_master, out_first, out_second, out_rollout, rollout, whole_sem, part_sem):
    x, y, z, _ = place()
    rows = new_master.shape[0]
    count = NX * 2 * NZ
    wholes = [
        pltpu.make_async_copy(src, dst, whole_sem.at[i])
        for i, (src, dst) in enumerate(((new_master, out_master), (new_first, out_first), (new_second, out_second)))
    ]

    def block(i, k):
        dx, dz = offset(k)
        pool, fsdp, _ = device(x + NX - dx, y + NY - i, z + NZ - dz, 0)
        start = pl.multiple_of((pool * count + fsdp) * (2 * rows), 2 * rows)
        parts = []
        for c in (0, 1):
            value = held[c, 1 + i, k].astype(jnp.float32)
            parts.append(jnp.concatenate([value[:rows], value[rows:]], axis=1))
        rollout[pl.ds(start, 2 * rows), :] = jnp.concatenate(parts, axis=0).astype(jnp.bfloat16)

    def part(j, pool):
        _, dz = offset(j * NX)
        size = NX * 2 * 2 * rows
        where = pl.ds(pl.multiple_of((pool * NZ + (z + NZ - dz) % NZ) * size, size), size)
        return pltpu.make_async_copy(rollout.at[where], out_rollout.at[where], part_sem.at[j, pool])

    for copy in wholes:
        copy.start()
    for j in range(NZ):

        def blocks(n, carry):
            for i in range(NY):
                block(i, j * NX + n)
            return carry

        lax.fori_loop(0, NX, blocks, 0)
        for pool in (0, 1):
            part(j, pool).start()
    for copy in wholes:
        copy.wait()
    for j in range(NZ):
        for pool in (0, 1):
            part(j, pool).wait()


def per_device(master, grad, first_moment, second_moment, matching):
    rows, width = master.shape
    count = matching.shape[0]
    cols = width // count
    total = 2 * count * 2 * rows
    hbm = pl.BlockSpec(memory_space=pltpu.HBM)
    pin = functools.partial(pltpu.with_memory_space_constraint, memory_space=pltpu.HBM)
    vmem = pl.BlockSpec(memory_space=pltpu.VMEM)
    dma = pltpu.SemaphoreType.DMA
    results = pl.pallas_call(
        kernel,
        out_shape=[pltpu.VMEM((rows, width), jnp.float32)] * 3 + [pltpu.VMEM((2, 1 + NY, STEPS, 2 * rows, cols // 2), jnp.bfloat16)],
        in_specs=[hbm] * 5,
        out_specs=[vmem] * 4,
        scratch_shapes=[
            pltpu.VMEM((rows, width), jnp.float32),
            pltpu.VMEM((rows, width), jnp.bfloat16),
            pltpu.VMEM((rows, width), jnp.float32),
            pltpu.VMEM((rows, width), jnp.float32),
            pltpu.VMEM((count, 2 * rows, cols // 2), jnp.bfloat16),
            pltpu.VMEM((1, count), jnp.int32),
            pltpu.VMEM((1, count), jnp.int32),
            pltpu.SMEM((1, count), jnp.int32),
            pltpu.VMEM((STEPS, 2, 2 * rows, cols // 2), jnp.bfloat16),
            dma((4, CHUNKS)),
            dma,
            dma,
            dma((len(GROUPS),)),
            dma((3,)),
            dma((3, len(GROUPS) + 1)),
            dma,
            dma((NZ,)),
            dma,
            dma,
            pltpu.SemaphoreType.REGULAR((4,)),
            pltpu.SemaphoreType.REGULAR((4,)),
        ],
        compiler_params=pltpu.CompilerParams(collective_id=0, has_side_effects=True, vmem_limit_bytes=20 << 20),
    )(*map(pin, (master, grad, first_moment, second_moment, matching.reshape(1, count))))
    new_master, new_first, new_second, rollout = pl.pallas_call(
        write,
        out_shape=[jax.ShapeDtypeStruct((rows, width), jnp.float32)] * 3 + [jax.ShapeDtypeStruct((total, cols), jnp.bfloat16)],
        in_specs=[vmem] * 4,
        out_specs=[hbm] * 4,
        scratch_shapes=[pltpu.VMEM((total, cols), jnp.bfloat16), dma((3,)), dma((NZ, 2))],
        compiler_params=pltpu.CompilerParams(vmem_limit_bytes=8 << 20),
    )(*(pltpu.with_memory_space_constraint(r, pltpu.VMEM) for r in results))
    return new_master, new_first, new_second, rollout.reshape(1, total, cols)


def solution(mesh):
    rows = P(("pool", "fsdp", "rep"), None)
    return jax.shard_map(
        per_device,
        mesh=mesh,
        in_specs=(rows, rows, rows, rows, P()),
        out_specs=(rows, rows, rows, P("fsdp", None, None)),
        check_vma=False,
    )
```
